32 devices in a mesh: dp: 4 (over y, x), lat: 4 (over z), lon: 2 (over core).
Axes of the slice: x: 2, y: 2, z: 4, core: 2. Of those that a mesh axis runs over, the one named last changes fastest.
Arguments:
- grid_feat: bfloat16 [128, 512, 474], P(('dp', 'lat'), 'lon'), parts along dimension 0, may hold values from -6 to 6
- mesh_in: bfloat16 [256, 64, 512], P(('dp', 'lat'), 'lon'), parts along dimension 0, may hold values from -6 to 6
- w_grid: bfloat16 [474, 512], replicated, may hold values from -0.25 to 0.25
- w_src: bfloat16 [512, 512], replicated, may hold values from -0.25 to 0.25
- w_dst: bfloat16 [512, 512], replicated, may hold values from -0.25 to 0.25
- b_edge: float32 [512], replicated, may hold values from -3 to 3
- w_node: bfloat16 [512, 512], replicated, may hold values from -0.25 to 0.25
- node_gain: float32 [512], replicated, may hold values from 0.5 to 1.5
- mix_gain: float32 [512], replicated, may hold values from 0.2 to 0.8
- send_rows: int32 [32, 8, 256], P(('dp', 'lat', 'lon')), parts along dimension 0, may hold values from 0 to 2047
- send_target: int32 [32, 8, 256], P(('dp', 'lat', 'lon')), parts along dimension 0, may hold values from 0 to 511
- send_counts: int32 [32, 8], P(('dp', 'lat', 'lon')), parts along dimension 0, may hold values from 0 to 256, as said below
- local_rows: int32 [32, 2048], P(('dp', 'lat', 'lon')), parts along dimension 0, may hold values from 0 to 2047
- local_target: int32 [32, 2048], P(('dp', 'lat', 'lon')), parts along dimension 0, may hold values from 0 to 511
- local_counts: int32 [32], P(('dp', 'lat', 'lon')), parts along dimension 0, may hold values from 1024 to 2048, as said below
- cotangent: bfloat16 [256, 64, 512], P(('dp', 'lat'), 'lon'), parts along dimension 0, may hold values from -6 to 6
Outputs:
- mesh_out: float32 [256, 64, 512], P(('dp', 'lat'), 'lon'), parts along dimension 0
- grad_grid: float32 [1896, 512], P('dp', ('lat', 'lon')), parts along dimension 0
- grad_src: float32 [2048, 512], P('dp', ('lat', 'lon')), parts along dimension 0
- grad_dst: float32 [2048, 512], P('dp', ('lat', 'lon')), parts along dimension 0
- grad_node: float32 [2048, 512], P('dp', ('lat', 'lon')), parts along dimension 0
The draws below stay inside these ranges and needn't reach their ends.
There are 4 independent parts, one for each index of `dp`. The reference program is written for one: setup_inputs(seed, part) draws one part's arguments, and reference() takes and returns one part's arrays. A program takes and returns all parts, laid end to end along the dimension named above; an argument that names none is the same for every part. Nothing has to cross between parts.
Inputs may be any that keep to these rules, and one draw needn't show every extreme that they name: send_counts[s, p] is the number of leading slots of send_rows[s, p] and send_target[s, p] that are edges; it is 0 unless p differs from s and the latitude indices of the tiles differ by at most one and their longitude indices by at most one around the cycle; it equals 256 somewhere in every draw. local_counts[p] is the number of leading entries of local_rows[p] and local_target[p] that are edges; it equals 2048 somewhere in every draw.
All inputs are finite; a program needn't handle non-finite values.
Results may differ from the reference program's by a relative error of at most 0.015.
Values may be sent and summed in bfloat16 or wider, within the bound.
A program may use at most 128 MiB of HBM per device.

```python
import jax
import jax.numpy as jnp
import numpy as np
from jax import lax

C = 474
L = 512
RLAT = 8
RLON = 256
MLAT = 16
MLON = 32
CAP = 256
EL = 2048
PEERS = 8
GLAT = 32
GLON = 512
MESH_LAT = 64
MESH_LON = 64
N_LAT = 4
N_LON = 2


def draw_send_counts(key, part):
    peer_count = N_LAT * N_LON
    source_tile = jnp.arange(peer_count, dtype=jnp.int32)[:, None]
    target_tile = jnp.arange(peer_count, dtype=jnp.int32)[None, :]
    source_lat = source_tile // N_LON
    target_lat = target_tile // N_LON
    lon_gap = (target_tile % N_LON - source_tile % N_LON) % N_LON
    nearby = (jnp.abs(target_lat - source_lat) <= 1) & ((lon_gap <= 1) | (lon_gap == N_LON - 1)) & (source_tile != target_tile)
    polar = (source_lat == 0) | (source_lat == N_LAT - 1)
    first_key, second_key, third_key = jax.random.split(jax.random.fold_in(key, 7), 3)
    heavy = jax.random.randint(first_key, (peer_count, peer_count), CAP // 2, CAP + 1)
    light = jax.random.randint(second_key, (peer_count, peer_count), CAP // 8, CAP // 2 + 1)
    counts = jnp.where(polar, heavy, light)
    chosen = jax.random.randint(third_key, (), 0, peer_count)
    chosen_lat = chosen // N_LON
    partner_lat = jnp.where(chosen_lat + 1 < N_LAT, chosen_lat + 1, chosen_lat - 1)
    partner = partner_lat * N_LON + chosen % N_LON
    counts = jnp.where((source_tile == chosen) & (target_tile == partner), CAP, counts)
    return jnp.where(nearby, counts, 0).astype(jnp.int32)


def draw_local_counts(key, part):
    peer_count = N_LAT * N_LON
    first_key, second_key = jax.random.split(jax.random.fold_in(key, 11))
    counts = jax.random.randint(first_key, (peer_count,), EL // 2, EL + 1)
    chosen = jax.random.randint(second_key, (), 0, peer_count)
    return jnp.where(jnp.arange(peer_count, dtype=jnp.int32) == chosen, EL, counts).astype(jnp.int32)


def plant(array, stream_key, least, high):
    longest = array.shape.index(max(array.shape))
    spots = []
    for shift in (0, 1):
        where = [jax.random.randint(jax.random.fold_in(stream_key, axis), (), 0, length) for axis, length in enumerate(array.shape)]
        where[longest] = (where[longest] + shift) % array.shape[longest]
        spots.append(tuple(where))
    return array.at[spots[0]].set(least).at[spots[1]].set(high)


def level_of(stream_key, dims, pieces, smallest, largest):
    gain, own = 1.0, jax.random.fold_in(stream_key, 6)
    for dim, blocks in pieces:
        steps = jnp.exp(jax.random.uniform(jax.random.fold_in(own, dim), (blocks,), jnp.float32, smallest / len(pieces), largest / len(pieces)))
        gain = gain * jnp.repeat(steps, dims[dim] // blocks).reshape([-1 if axis == dim else 1 for axis in range(len(dims))])
    return gain


def noise(key, dims, scale, most, cuts=(), kind=jnp.bfloat16):
    loudness = level_of(key, dims, cuts, -0.22, 0.18) if cuts else 1.0
    array = jax.random.normal(key, dims, jnp.float32) * scale * loudness
    return jnp.minimum(jnp.maximum(array, -most), most).astype(kind)


def setup_inputs(seed: int = 0, part: int = 0) -> dict:
    keys = jax.random.split(jax.random.key(seed), 17)
    part_keys = jax.random.split(jax.random.fold_in(keys[16], part), 17)
    grid_feat = noise(part_keys[0], (GLAT, GLON, C), 1.0, 6.0, ((0, 4), (1, 2)))
    mesh_in = noise(part_keys[1], (MESH_LAT, MESH_LON, L), 1.0, 6.0, ((0, 4), (1, 2)))
    w_grid = noise(keys[2], (C, L), C ** -0.5, 0.25)
    w_src = noise(keys[3], (L, L), L ** -0.5, 0.25)
    w_dst = noise(keys[4], (L, L), L ** -0.5, 0.25)
    b_edge = noise(keys[5], (L,), 0.5, 3.0, (), jnp.float32)
    w_node = noise(keys[6], (L, L), L ** -0.5, 0.25)
    node_gain = jnp.clip(1.0 + 0.1 * jax.random.normal(keys[7], (L,), jnp.float32), 0.5, 1.5)
    mix_gain = jnp.clip(jax.random.uniform(keys[8], (L,), jnp.float32, 0.2, 0.8), 0.2, 0.8)
    send_rows = plant(jax.random.randint(part_keys[9], (PEERS, PEERS, CAP), 0, RLAT * RLON), jax.random.fold_in(part_keys[9], 1), 0, (RLAT * RLON) - 1).astype(jnp.int32)
    send_target = plant(jax.random.randint(part_keys[10], (PEERS, PEERS, CAP), 0, MLAT * MLON), jax.random.fold_in(part_keys[10], 1), 0, (MLAT * MLON) - 1).astype(jnp.int32)
    send_counts = draw_send_counts(jax.random.fold_in(jax.random.fold_in(keys[16], part), 71), part)
    local_rows = plant(jax.random.randint(part_keys[12], (PEERS, EL), 0, RLAT * RLON), jax.random.fold_in(part_keys[12], 1), 0, (RLAT * RLON) - 1).astype(jnp.int32)
    local_target = plant(jax.random.randint(part_keys[13], (PEERS, EL), 0, MLAT * MLON), jax.random.fold_in(part_keys[13], 1), 0, (MLAT * MLON) - 1).astype(jnp.int32)
    local_counts = draw_local_counts(jax.random.fold_in(jax.random.fold_in(keys[16], part), 71), part)
    cotangent = noise(part_keys[15], (MESH_LAT, MESH_LON, L), 1.0, 6.0, ((0, 4), (1, 2)))
    return {"grid_feat": grid_feat, "mesh_in": mesh_in, "w_grid": w_grid, "w_src": w_src, "w_dst": w_dst, "b_edge": b_edge, "w_node": w_node, "node_gain": node_gain, "mix_gain": mix_gain, "send_rows": send_rows, "send_target": send_target, "send_counts": send_counts, "local_rows": local_rows, "local_target": local_target, "local_counts": local_counts, "cotangent": cotangent}


LAYER_EPSILON = 1e-05

def silu_slope(values):
    sigmoid_part = jax.nn.sigmoid(values)
    return sigmoid_part * (1.0 + values * (1.0 - sigmoid_part))

def tiles_first(whole, tile_a, tile_b):
    channels = whole.shape[-1]
    blocks = whole.reshape(N_LAT, tile_a, N_LON, tile_b, channels)
    return blocks.transpose(0, 2, 1, 3, 4).reshape(N_LAT * N_LON, tile_a * tile_b, channels)

def tiles_back(tiled, tile_a, tile_b):
    channels = tiled.shape[-1]
    blocks = tiled.reshape(N_LAT, N_LON, tile_a, tile_b, channels)
    return blocks.transpose(0, 2, 1, 3, 4).reshape(N_LAT * tile_a, N_LON * tile_b, channels)

def cycle_mix(mesh_field):
    above = jnp.pad(mesh_field[1:], ((0, 1), (0, 0), (0, 0)))
    below = jnp.pad(mesh_field[:-1], ((1, 0), (0, 0), (0, 0)))
    return 0.25 * (above + below + jnp.roll(mesh_field, 1, axis=1) + jnp.roll(mesh_field, -1, axis=1))

def neighbour_table():
    lat_steps = [lat_step for lat_step in (-1, 0, 1) if abs(lat_step) < N_LAT]
    lon_steps = sorted(set((lon_step % N_LON for lon_step in (-1, 0, 1))))
    offsets = [(lat_step, lon_step) for lat_step in lat_steps for lon_step in lon_steps if (lat_step, lon_step) != (0, 0)]
    peer_count = N_LAT * N_LON
    source_table = np.zeros((peer_count, len(offsets)), np.int32)
    usable = np.zeros((peer_count, len(offsets)), np.float32)
    for target_tile in range(peer_count):
        tile_row = target_tile // N_LON
        tile_column = target_tile % N_LON
        for position, (lat_step, lon_step) in enumerate(offsets):
            source_row = tile_row - lat_step
            if 0 <= source_row < N_LAT:
                source_table[target_tile, position] = source_row * N_LON + (tile_column - lon_step) % N_LON
                usable[target_tile, position] = 1.0
    return (source_table, usable)

def reference(grid_feat, mesh_in, w_grid, w_src, w_dst, b_edge, w_node, node_gain, mix_gain, send_rows, send_target, send_counts, local_rows, local_target, local_counts, cotangent):
    peer_count = N_LAT * N_LON
    tile_rows = RLAT * RLON
    tile_nodes = MLAT * MLON
    features = tiles_first(grid_feat, RLAT, RLON).reshape(-1, C)
    mesh_tiles = tiles_first(mesh_in, MLAT, MLON)
    mesh_flat = mesh_tiles.reshape(-1, L)
    grid_pre = jnp.dot(features, w_grid, preferred_element_type=jnp.float32)
    grid_latent = jax.nn.silu(grid_pre).astype(jnp.bfloat16)
    queries = jnp.dot(mesh_flat, w_dst, preferred_element_type=jnp.float32).reshape(peer_count, tile_nodes, L)
    source_table, usable = neighbour_table()
    remote_sources = jnp.asarray(source_table).astype(jnp.int32)
    usable_tiles = jnp.asarray(usable).astype(jnp.float32)
    dest_ids = jnp.arange(peer_count, dtype=jnp.int32)
    slot_ids = jnp.arange(CAP, dtype=jnp.int32)
    local_senders = dest_ids[:, None] * tile_rows + local_rows
    local_valid = (jnp.arange(EL, dtype=jnp.int32)[None, :] < local_counts[:, None]).astype(jnp.float32)
    remote_rows = send_rows[remote_sources, dest_ids[:, None], :]
    remote_senders = remote_sources[:, :, None] * tile_rows + remote_rows
    remote_targets = send_target[remote_sources, dest_ids[:, None], :]
    remote_counts = send_counts[remote_sources, dest_ids[:, None]]
    remote_valid = (slot_ids[None, None, :] < remote_counts[:, :, None]).astype(jnp.float32) * usable_tiles[:, :, None]
    edge_senders = jnp.concatenate([local_senders, remote_senders.reshape(peer_count, -1)], axis=1).astype(jnp.int32)
    edge_targets = jnp.concatenate([local_target, remote_targets.reshape(peer_count, -1)], axis=1).astype(jnp.int32)
    edge_mask = jnp.concatenate([local_valid, remote_valid.reshape(peer_count, -1)], axis=1)

    def messages_of(senders, targets, valid, query_tile):
        gathered = grid_latent[senders]
        pre_edge = jnp.dot(gathered, w_src, preferred_element_type=jnp.float32) + query_tile[targets] + b_edge
        message = (jax.nn.silu(pre_edge) * valid[:, None]).astype(jnp.bfloat16)
        return (gathered, pre_edge, message)

    def forward_tile(packed):
        senders, targets, valid, query_tile = packed
        message = messages_of(senders, targets, valid, query_tile)[2]
        return jax.ops.segment_sum(message.astype(jnp.float32), targets, num_segments=tile_nodes)
    aggregate = lax.map(forward_tile, (edge_senders, edge_targets, edge_mask, queries))
    aggregate_b = aggregate.reshape(-1, L).astype(jnp.bfloat16)
    hidden = jnp.dot(aggregate_b, w_node, preferred_element_type=jnp.float32)
    active = jax.nn.silu(hidden)
    row_mean = lax.optimization_barrier(jnp.mean(active, axis=-1, keepdims=True))
    centred = active - row_mean
    inverse_scale = lax.rsqrt(lax.optimization_barrier(jnp.mean(centred * centred, axis=-1, keepdims=True)) + LAYER_EPSILON)
    normed = centred * inverse_scale
    updated = (mesh_flat.astype(jnp.float32) + normed * node_gain).astype(jnp.bfloat16)
    updated_field = tiles_back(updated.reshape(peer_count, tile_nodes, L), MLAT, MLON).astype(jnp.float32)
    mesh_out = updated_field + mix_gain * cycle_mix(updated_field)
    cot_values = cotangent.astype(jnp.float32)
    mixed_cot = (mix_gain * cot_values).astype(jnp.bfloat16)
    d_updated = cot_values + cycle_mix(mixed_cot.astype(jnp.float32))
    scaled_grad = tiles_first(d_updated, MLAT, MLON).reshape(-1, L) * node_gain
    d_active = inverse_scale * (scaled_grad - lax.optimization_barrier(jnp.mean(scaled_grad, axis=-1, keepdims=True)) - normed * lax.optimization_barrier(jnp.mean(scaled_grad * normed, axis=-1, keepdims=True)))
    d_hidden = (d_active * silu_slope(hidden)).astype(jnp.bfloat16)
    grad_node = jnp.dot(aggregate_b.T, d_hidden, preferred_element_type=jnp.float32)
    d_aggregate = jnp.dot(d_hidden, w_node.T, preferred_element_type=jnp.float32).astype(jnp.bfloat16).reshape(peer_count, tile_nodes, L)

    def backward_tile(packed):
        senders, targets, valid, query_tile, d_agg_tile = packed
        gathered, pre_edge, unused_message = messages_of(senders, targets, valid, query_tile)
        d_message = d_agg_tile[targets]
        d_pre = (d_message.astype(jnp.float32) * silu_slope(pre_edge) * valid[:, None]).astype(jnp.bfloat16)
        grad_part = jnp.dot(gathered.T, d_pre, preferred_element_type=jnp.float32)
        d_gathered = jnp.dot(d_pre, w_src.T, preferred_element_type=jnp.float32).astype(jnp.bfloat16)
        d_query = jax.ops.segment_sum(d_pre.astype(jnp.float32), targets, num_segments=tile_nodes).astype(jnp.bfloat16)
        return (grad_part, d_gathered, d_query)
    grad_parts, d_gathered, d_query = lax.map(backward_tile, (edge_senders, edge_targets, edge_mask, queries, d_aggregate))
    grad_src = lax.optimization_barrier(jnp.sum(grad_parts, axis=0))
    grad_dst = jnp.dot(mesh_flat.T, d_query.reshape(-1, L), preferred_element_type=jnp.float32)
    d_grid = jax.ops.segment_sum(d_gathered.reshape(-1, L).astype(jnp.float32), edge_senders.reshape(-1), num_segments=peer_count * tile_rows)
    d_grid_pre = (d_grid * silu_slope(grid_pre)).astype(jnp.bfloat16)
    grad_grid = jnp.dot(features.T, d_grid_pre, preferred_element_type=jnp.float32)
    return (mesh_out, grad_grid, grad_src, grad_dst, grad_node)
```

```python
import jax
import jax.numpy as jnp
from jax import lax
from jax.sharding import PartitionSpec as P

LAYER_EPSILON = 1e-05


def tile_route(lat_count, lon_count, lat_step, lon_step):
    return [
        (i * lon_count + j, (i + lat_step) * lon_count + (j + lon_step) % lon_count)
        for i in range(lat_count)
        for j in range(lon_count)
        if 0 <= i + lat_step < lat_count
    ]


def moved(block, lat_step, lon_step):
    route = tile_route(lax.axis_size("lat"), lax.axis_size("lon"), lat_step, lon_step)
    return lax.ppermute(block, ("lat", "lon"), route)


def silu_slope(values):
    sigmoid_part = jax.nn.sigmoid(values)
    return sigmoid_part * (1.0 + values * (1.0 - sigmoid_part))


def product(left_rows, right_rows):
    return jnp.dot(left_rows, right_rows, preferred_element_type=jnp.float32)


def inner_rows(left_rows, right_rows):
    return lax.dot_general(
        left_rows, right_rows, (((0,), (0,)), ((), ())), preferred_element_type=jnp.float32
    )


def against_rows(left_rows, right_rows):
    return lax.dot_general(
        left_rows, right_rows, (((1,), (1,)), ((), ())), preferred_element_type=jnp.float32
    )


def neighbour_offsets(lat_count, lon_count):
    lat_steps = [lat_step for lat_step in (-1, 0, 1) if abs(lat_step) < lat_count]
    lon_steps = sorted(set((lon_step % lon_count for lon_step in (-1, 0, 1))))
    return [
        (lat_step, lon_step)
        for lat_step in lat_steps
        for lon_step in lon_steps
        if (lat_step, lon_step) != (0, 0)
    ]


def border_sides(lat_step, lon_step, lon_count):
    if lon_step == 0:
        return [(0, "last" if lat_step > 0 else "first")]
    if lat_step != 0:
        return []
    sides = []
    if lon_step == 1:
        sides.append((1, "last"))
    if lon_step == lon_count - 1:
        sides.append((1, "first"))
    return sides


def border_of(field, side):
    dim, end = side
    at = 0 if end == "first" else field.shape[dim] - 1
    return lax.index_in_dim(field, at, dim, keepdims=False)


def neighbour_mix(field, halos):
    field = field.astype(jnp.float32)
    halos = {side: halo.astype(jnp.float32) for side, halo in halos.items()}
    up = jnp.concatenate([field[1:], halos[(0, "first")][None]], axis=0)
    down = jnp.concatenate([halos[(0, "last")][None], field[:-1]], axis=0)
    right = jnp.concatenate([field[:, 1:], halos[(1, "first")][:, None]], axis=1)
    left = jnp.concatenate([halos[(1, "last")][:, None], field[:, :-1]], axis=1)
    return 0.25 * (up + down + right + left)


def one_hot(indices, count):
    return (indices[:, None] == jnp.arange(count, dtype=jnp.int32)[None, :]).astype(jnp.bfloat16)


def on_device(
    grid_feat,
    mesh_in,
    w_grid,
    w_src,
    w_dst,
    b_edge,
    w_node,
    node_gain,
    mix_gain,
    send_rows,
    send_target,
    send_counts,
    local_rows,
    local_target,
    local_counts,
    cotangent,
):
    lat_count = lax.axis_size("lat")
    lon_count = lax.axis_size("lon")
    lat_index = lax.axis_index("lat")
    lon_index = lax.axis_index("lon")
    tile_a, tile_b, channels = grid_feat.shape
    mesh_a, mesh_b, latent = mesh_in.shape
    tile_rows = tile_a * tile_b
    tile_nodes = mesh_a * mesh_b
    capacity = send_rows.shape[2]
    local_slots = local_rows.shape[1]
    features = grid_feat.reshape(tile_rows, channels)
    mesh_flat = mesh_in.reshape(tile_nodes, latent)
    offsets = neighbour_offsets(lat_count, lon_count)
    slot_ids = jnp.arange(capacity, dtype=jnp.int32)
    target_codes = jnp.where(slot_ids[None, :] < send_counts[0][:, None], send_target[0] + 1, 0)
    chosen_rows, code_rows = [], []
    code_height = -(-2 * capacity // latent)
    for lat_step, lon_step in offsets:
        target_tile = (
            jnp.clip(lat_index + lat_step, 0, lat_count - 1) * lon_count
            + (lon_index + lon_step) % lon_count
        )
        chosen_rows.append(lax.dynamic_index_in_dim(send_rows[0], target_tile, 0, keepdims=False))
        codes = lax.dynamic_index_in_dim(target_codes, target_tile, 0, keepdims=False)
        halves = jnp.concatenate([codes // 256, codes % 256]).astype(jnp.bfloat16)
        halves = jnp.pad(halves, (0, code_height * latent - 2 * capacity))
        code_rows.append(halves.reshape(code_height, latent))
    sent_rows = jnp.concatenate(chosen_rows)
    mixed_cot = (mix_gain * cotangent.astype(jnp.float32)).astype(jnp.bfloat16)

    grid_pre = product(features, w_grid)
    grid_latent = jax.nn.silu(grid_pre).astype(jnp.bfloat16)
    sent_latent = product(one_hot(sent_rows, tile_rows), grid_latent).astype(jnp.bfloat16)

    arrived_blocks, arrived_codes, cot_halos = [], [], {}
    for p, (lat_step, lon_step) in enumerate(offsets):
        sides = border_sides(lat_step, lon_step, lon_count)
        pieces = [sent_latent[p * capacity : (p + 1) * capacity], code_rows[p]]
        pieces += [border_of(mixed_cot, side) for side in sides]
        came = moved(jnp.concatenate(pieces, axis=0), lat_step, lon_step)
        arrived_blocks.append(came[:capacity])
        halves = came[capacity : capacity + code_height].reshape(-1)[: 2 * capacity]
        halves = halves.astype(jnp.int32)
        arrived_codes.append(halves[:capacity] * 256 + halves[capacity:])
        at = capacity + code_height
        for side in sides:
            height = mixed_cot.shape[1 - side[0]]
            cot_halos[side] = came[at : at + height]
            at += height

    queries = (product(mesh_flat, w_dst) + b_edge).astype(jnp.bfloat16)
    here_valid = jnp.arange(local_slots, dtype=jnp.int32) < local_counts[0]
    here_targets = jnp.where(here_valid, local_target[0], -1)
    here_rows = local_rows[0]
    here_latent = product(one_hot(here_rows, tile_rows), grid_latent).astype(jnp.bfloat16)

    def edge_inputs(edge_latent, targets):
        return product(edge_latent, w_src) + product(one_hot(targets, tile_nodes), queries)

    def edge_sums(pre_edge, targets):
        return inner_rows(one_hot(targets, tile_nodes), jax.nn.silu(pre_edge).astype(jnp.bfloat16))

    here_pre = edge_inputs(here_latent, here_targets)
    here_sums = edge_sums(here_pre, here_targets)
    far_latent = jnp.concatenate(arrived_blocks, axis=0)
    far_targets = jnp.concatenate(arrived_codes) - 1
    far_pre = edge_inputs(far_latent, far_targets)
    aggregate = here_sums + edge_sums(far_pre, far_targets)

    aggregate_b = aggregate.astype(jnp.bfloat16)
    hidden = product(aggregate_b, w_node)
    active = jax.nn.silu(hidden)
    row_mean = jnp.mean(active, axis=-1, keepdims=True)
    centred = active - row_mean
    inverse_scale = lax.rsqrt(jnp.mean(centred * centred, axis=-1, keepdims=True) + LAYER_EPSILON)
    normed = centred * inverse_scale
    updated = (
        (mesh_flat.astype(jnp.float32) + normed * node_gain)
        .astype(jnp.bfloat16)
        .reshape(mesh_a, mesh_b, latent)
    )
    d_updated = cotangent.astype(jnp.float32) + neighbour_mix(mixed_cot, cot_halos)
    scaled_grad = d_updated.reshape(tile_nodes, latent) * node_gain
    d_active = inverse_scale * (
        scaled_grad
        - jnp.mean(scaled_grad, axis=-1, keepdims=True)
        - normed * jnp.mean(scaled_grad * normed, axis=-1, keepdims=True)
    )
    d_hidden = (d_active * silu_slope(hidden)).astype(jnp.bfloat16)
    d_aggregate = against_rows(d_hidden, w_node).astype(jnp.bfloat16)

    def edge_grads(pre_edge, targets):
        d_message = product(one_hot(targets, tile_nodes), d_aggregate)
        return (d_message.astype(jnp.bfloat16) * silu_slope(pre_edge)).astype(jnp.bfloat16)

    far_d_pre = edge_grads(far_pre, far_targets)
    far_d_latent = against_rows(far_d_pre, w_src).astype(jnp.bfloat16)
    returned, halos = [], {}
    for p, (lat_step, lon_step) in enumerate(offsets):
        back = (-lat_step, (-lon_step) % lon_count)
        sides = border_sides(back[0], back[1], lon_count)
        pieces = [far_d_latent[p * capacity : (p + 1) * capacity]]
        pieces += [border_of(updated, side) for side in sides]
        came = moved(jnp.concatenate(pieces, axis=0), back[0], back[1])
        returned.append(came[:capacity])
        at = capacity
        for side in sides:
            height = updated.shape[1 - side[0]]
            halos[side] = came[at : at + height]
            at += height

    def scattered(grad):
        return lax.psum_scatter(grad, ("lat", "lon"), scatter_dimension=1, tiled=True)

    grad_node = scattered(inner_rows(aggregate_b, d_hidden))
    here_d_pre = edge_grads(here_pre, here_targets)
    grad_src = scattered(inner_rows(here_latent, here_d_pre) + inner_rows(far_latent, far_d_pre))
    d_query = inner_rows(one_hot(here_targets, tile_nodes), here_d_pre) + inner_rows(
        one_hot(far_targets, tile_nodes), far_d_pre
    )
    grad_dst = scattered(inner_rows(mesh_flat, d_query.astype(jnp.bfloat16)))
    here_d_latent = against_rows(here_d_pre, w_src).astype(jnp.bfloat16)
    d_grid = inner_rows(one_hot(here_rows, tile_rows), here_d_latent) + inner_rows(
        one_hot(sent_rows, tile_rows), jnp.concatenate(returned, axis=0)
    )
    d_grid_pre = (d_grid * silu_slope(grid_pre)).astype(jnp.bfloat16)
    grad_grid = scattered(inner_rows(features, d_grid_pre))
    mesh_out = updated.astype(jnp.float32) + mix_gain * neighbour_mix(updated, halos)
    return (mesh_out, grad_grid, grad_src, grad_dst, grad_node)


def solution(mesh):
    return jax.shard_map(
        on_device,
        mesh=mesh,
        in_specs=(
            P(("dp", "lat"), "lon", None),
            P(("dp", "lat"), "lon", None),
            P(),
            P(),
            P(),
            P(),
            P(),
            P(),
            P(),
            P(("dp", "lat", "lon"), None, None),
            P(("dp", "lat", "lon"), None, None),
            P(("dp", "lat", "lon"), None),
            P(("dp", "lat", "lon"), None),
            P(("dp", "lat", "lon"), None),
            P(("dp", "lat", "lon")),
            P(("dp", "lat"), "lon", None),
        ),
        out_specs=(
            P(("dp", "lat"), "lon", None),
            P("dp", ("lat", "lon")),
            P("dp", ("lat", "lon")),
            P("dp", ("lat", "lon")),
            P("dp", ("lat", "lon")),
        ),
        check_vma=False,
    )
```

```python
import jax
import jax.numpy as jnp
from jax import lax
from jax.sharding import PartitionSpec as P

LAYER_EPSILON = 1e-05


def tile_route(lat_count, lon_count, lat_step, lon_step):
    return [
        (i * lon_count + j, (i + lat_step) * lon_count + (j + lon_step) % lon_count)
        for i in range(lat_count)
        for j in range(lon_count)
        if 0 <= i + lat_step < lat_count
    ]


def moved(block, lat_step, lon_step):
    route = tile_route(lax.axis_size("lat"), lax.axis_size("lon"), lat_step, lon_step)
    return lax.ppermute(block, ("lat", "lon"), route)


def silu_slope(values):
    sigmoid_part = jax.nn.sigmoid(values)
    return sigmoid_part * (1.0 + values * (1.0 - sigmoid_part))


def product(left_rows, right_rows):
    return jnp.dot(left_rows, right_rows, preferred_element_type=jnp.float32)


def inner_rows(left_rows, right_rows):
    return lax.dot_general(
        left_rows, right_rows, (((0,), (0,)), ((), ())), preferred_element_type=jnp.float32
    )


def against_rows(left_rows, right_rows):
    return lax.dot_general(
        left_rows, right_rows, (((1,), (1,)), ((), ())), preferred_element_type=jnp.float32
    )


def neighbour_offsets(lat_count, lon_count):
    lat_steps = [lat_step for lat_step in (-1, 0, 1) if abs(lat_step) < lat_count]
    lon_steps = sorted(set((lon_step % lon_count for lon_step in (-1, 0, 1))))
    return [
        (lat_step, lon_step)
        for lat_step in lat_steps
        for lon_step in lon_steps
        if (lat_step, lon_step) != (0, 0)
    ]


def border_sides(lat_step, lon_step, lon_count):
    if lon_step == 0:
        return [(0, "last" if lat_step > 0 else "first")]
    if lat_step != 0:
        return []
    sides = []
    if lon_step == 1:
        sides.append((1, "last"))
    if lon_step == lon_count - 1:
        sides.append((1, "first"))
    return sides


def border_of(field, side):
    dim, end = side
    at = 0 if end == "first" else field.shape[dim] - 1
    return lax.index_in_dim(field, at, dim, keepdims=False)


def neighbour_mix(field, halos):
    field = field.astype(jnp.float32)
    halos = {side: halo.astype(jnp.float32) for side, halo in halos.items()}
    up = jnp.concatenate([field[1:], halos[(0, "first")][None]], axis=0)
    down = jnp.concatenate([halos[(0, "last")][None], field[:-1]], axis=0)
    right = jnp.concatenate([field[:, 1:], halos[(1, "first")][:, None]], axis=1)
    left = jnp.concatenate([halos[(1, "last")][:, None], field[:, :-1]], axis=1)
    return 0.25 * (up + down + right + left)


def one_hot(indices, count):
    return (indices[:, None] == jnp.arange(count, dtype=jnp.int32)[None, :]).astype(jnp.bfloat16)


def shared_over(blocks, axis):
    count, index = lax.axis_size(axis), lax.axis_index(axis)
    total = lax.dynamic_index_in_dim(blocks, index, 0, keepdims=False).astype(jnp.float32)
    for step in range(1, count):
        block = lax.dynamic_index_in_dim(blocks, (index + step) % count, 0, keepdims=False)
        route = [(i, (i + step) % count) for i in range(count)]
        total += lax.ppermute(block.astype(jnp.bfloat16), axis, route).astype(jnp.float32)
    return total


def column_shares(grad):
    lat_count, lon_count = lax.axis_size("lat"), lax.axis_size("lon")
    blocks = grad.reshape(lat_count, lon_count, -1, grad.shape[1])
    return shared_over(shared_over(blocks.swapaxes(0, 1), "lon"), "lat")


def on_device(
    grid_feat,
    mesh_in,
    w_grid,
    w_src,
    w_dst,
    b_edge,
    w_node,
    node_gain,
    mix_gain,
    send_rows,
    send_target,
    send_counts,
    local_rows,
    local_target,
    local_counts,
    cotangent,
):
    lat_count = lax.axis_size("lat")
    lon_count = lax.axis_size("lon")
    lat_index = lax.axis_index("lat")
    lon_index = lax.axis_index("lon")
    tile_a, tile_b, channels = grid_feat.shape
    mesh_a, mesh_b, latent = mesh_in.shape
    tile_rows = tile_a * tile_b
    tile_nodes = mesh_a * mesh_b
    capacity = send_rows.shape[2]
    local_slots = local_rows.shape[1]
    features = grid_feat.reshape(tile_rows, channels)
    mesh_flat = mesh_in.reshape(tile_nodes, latent)
    offsets = neighbour_offsets(lat_count, lon_count)
    slot_ids = jnp.arange(capacity, dtype=jnp.int32)
    target_codes = jnp.where(slot_ids[None, :] < send_counts[0][:, None], send_target[0] + 1, 0)
    chosen_rows, code_rows = [], []
    code_height = -(-2 * capacity // latent)
    for lat_step, lon_step in offsets:
        target_tile = (
            jnp.clip(lat_index + lat_step, 0, lat_count - 1) * lon_count
            + (lon_index + lon_step) % lon_count
        )
        chosen_rows.append(lax.dynamic_index_in_dim(send_rows[0], target_tile, 0, keepdims=False))
        codes = lax.dynamic_index_in_dim(target_codes, target_tile, 0, keepdims=False)
        halves = jnp.concatenate([codes // 256, codes % 256]).astype(jnp.bfloat16)
        halves = jnp.pad(halves, (0, code_height * latent - 2 * capacity))
        code_rows.append(halves.reshape(code_height, latent))
    sent_rows = jnp.concatenate(chosen_rows)
    mixed_cot = (mix_gain * cotangent.astype(jnp.float32)).astype(jnp.bfloat16)

    grid_pre = product(features, w_grid)
    grid_latent = jax.nn.silu(grid_pre).astype(jnp.bfloat16)
    sent_latent = product(one_hot(sent_rows, tile_rows), grid_latent).astype(jnp.bfloat16)

    arrived_blocks, arrived_codes, cot_halos = [], [], {}
    for p, (lat_step, lon_step) in enumerate(offsets):
        sides = border_sides(lat_step, lon_step, lon_count)
        pieces = [sent_latent[p * capacity : (p + 1) * capacity], code_rows[p]]
        pieces += [border_of(mixed_cot, side) for side in sides]
        came = moved(jnp.concatenate(pieces, axis=0), lat_step, lon_step)
        arrived_blocks.append(came[:capacity])
        halves = came[capacity : capacity + code_height].reshape(-1)[: 2 * capacity]
        halves = halves.astype(jnp.int32)
        arrived_codes.append(halves[:capacity] * 256 + halves[capacity:])
        at = capacity + code_height
        for side in sides:
            height = mixed_cot.shape[1 - side[0]]
            cot_halos[side] = came[at : at + height]
            at += height

    queries = (product(mesh_flat, w_dst) + b_edge).astype(jnp.bfloat16)
    here_valid = jnp.arange(local_slots, dtype=jnp.int32) < local_counts[0]
    here_targets = jnp.where(here_valid, local_target[0], -1)
    here_rows = local_rows[0]
    here_latent = product(one_hot(here_rows, tile_rows), grid_latent).astype(jnp.bfloat16)

    def edge_inputs(edge_latent, targets):
        return product(edge_latent, w_src) + product(one_hot(targets, tile_nodes), queries)

    def edge_sums(pre_edge, targets):
        return inner_rows(one_hot(targets, tile_nodes), jax.nn.silu(pre_edge).astype(jnp.bfloat16))

    here_pre = edge_inputs(here_latent, here_targets)
    here_sums = edge_sums(here_pre, here_targets)
    far_latent = jnp.concatenate(arrived_blocks, axis=0)
    far_targets = jnp.concatenate(arrived_codes) - 1
    far_pre = edge_inputs(far_latent, far_targets)
    aggregate = here_sums + edge_sums(far_pre, far_targets)

    aggregate_b = aggregate.astype(jnp.bfloat16)
    hidden = product(aggregate_b, w_node)
    active = jax.nn.silu(hidden)
    row_mean = jnp.mean(active, axis=-1, keepdims=True)
    centred = active - row_mean
    inverse_scale = lax.rsqrt(jnp.mean(centred * centred, axis=-1, keepdims=True) + LAYER_EPSILON)
    normed = centred * inverse_scale
    updated = (
        (mesh_flat.astype(jnp.float32) + normed * node_gain)
        .astype(jnp.bfloat16)
        .reshape(mesh_a, mesh_b, latent)
    )
    d_updated = cotangent.astype(jnp.float32) + neighbour_mix(mixed_cot, cot_halos)
    scaled_grad = d_updated.reshape(tile_nodes, latent) * node_gain
    d_active = inverse_scale * (
        scaled_grad
        - jnp.mean(scaled_grad, axis=-1, keepdims=True)
        - normed * jnp.mean(scaled_grad * normed, axis=-1, keepdims=True)
    )
    d_hidden = (d_active * silu_slope(hidden)).astype(jnp.bfloat16)
    d_aggregate = against_rows(d_hidden, w_node).astype(jnp.bfloat16)

    def edge_grads(pre_edge, targets):
        d_message = product(one_hot(targets, tile_nodes), d_aggregate)
        return (d_message.astype(jnp.bfloat16) * silu_slope(pre_edge)).astype(jnp.bfloat16)

    far_d_pre = edge_grads(far_pre, far_targets)
    far_d_latent = against_rows(far_d_pre, w_src).astype(jnp.bfloat16)
    returned, halos = [], {}
    for p, (lat_step, lon_step) in enumerate(offsets):
        back = (-lat_step, (-lon_step) % lon_count)
        sides = border_sides(back[0], back[1], lon_count)
        pieces = [far_d_latent[p * capacity : (p + 1) * capacity]]
        pieces += [border_of(updated, side) for side in sides]
        came = moved(jnp.concatenate(pieces, axis=0), back[0], back[1])
        returned.append(came[:capacity])
        at = capacity
        for side in sides:
            height = updated.shape[1 - side[0]]
            halos[side] = came[at : at + height]
            at += height

    grad_node = inner_rows(d_hidden, aggregate_b)
    here_d_pre = edge_grads(here_pre, here_targets)
    grad_src = inner_rows(here_d_pre, here_latent) + inner_rows(far_d_pre, far_latent)
    d_query = inner_rows(one_hot(here_targets, tile_nodes), here_d_pre) + inner_rows(
        one_hot(far_targets, tile_nodes), far_d_pre
    )
    grad_dst = inner_rows(d_query.astype(jnp.bfloat16), mesh_flat)
    early = column_shares(jnp.concatenate([grad_node, grad_src, grad_dst], axis=1))
    here_d_latent = against_rows(here_d_pre, w_src).astype(jnp.bfloat16)
    d_grid = inner_rows(one_hot(here_rows, tile_rows), here_d_latent) + inner_rows(
        one_hot(sent_rows, tile_rows), jnp.concatenate(returned, axis=0)
    )
    d_grid_pre = (d_grid * silu_slope(grid_pre)).astype(jnp.bfloat16)
    grad_grid = column_shares(inner_rows(d_grid_pre, features)).T
    grad_node = early[:, :latent].T
    grad_src = early[:, latent : 2 * latent].T
    grad_dst = early[:, 2 * latent :].T
    mesh_out = updated.astype(jnp.float32) + mix_gain * neighbour_mix(updated, halos)
    return (mesh_out, grad_grid, grad_src, grad_dst, grad_node)


def solution(mesh):
    return jax.shard_map(
        on_device,
        mesh=mesh,
        in_specs=(
            P(("dp", "lat"), "lon", None),
            P(("dp", "lat"), "lon", None),
            P(),
            P(),
            P(),
            P(),
            P(),
            P(),
            P(),
            P(("dp", "lat", "lon"), None, None),
            P(("dp", "lat", "lon"), None, None),
            P(("dp", "lat", "lon"), None),
            P(("dp", "lat", "lon"), None),
            P(("dp", "lat", "lon"), None),
            P(("dp", "lat", "lon")),
            P(("dp", "lat"), "lon", None),
        ),
        out_specs=(
            P(("dp", "lat"), "lon", None),
            P("dp", ("lat", "lon")),
            P("dp", ("lat", "lon")),
            P("dp", ("lat", "lon")),
            P("dp", ("lat", "lon")),
        ),
        check_vma=False,
    )
```

```python
import jax
import jax.numpy as jnp
from jax import lax
from jax.sharding import PartitionSpec as P

LAYER_EPSILON = 1e-05


def tile_route(lat_count, lon_count, lat_step, lon_step):
    return [
        (i * lon_count + j, (i + lat_step) * lon_count + (j + lon_step) % lon_count)
        for i in range(lat_count)
        for j in range(lon_count)
        if 0 <= i + lat_step < lat_count
    ]


def moved(block, lat_step, lon_step):
    route = tile_route(lax.axis_size("lat"), lax.axis_size("lon"), lat_step, lon_step)
    return lax.ppermute(block, ("lat", "lon"), route)


def silu_slope(values):
    sigmoid_part = jax.nn.sigmoid(values)
    return sigmoid_part * (1.0 + values * (1.0 - sigmoid_part))


def product(left_rows, right_rows):
    return jnp.dot(left_rows, right_rows, preferred_element_type=jnp.float32)


def inner_rows(left_rows, right_rows):
    return lax.dot_general(
        left_rows, right_rows, (((0,), (0,)), ((), ())), preferred_element_type=jnp.float32
    )


def against_rows(left_rows, right_rows):
    return lax.dot_general(
        left_rows, right_rows, (((1,), (1,)), ((), ())), preferred_element_type=jnp.float32
    )


def neighbour_offsets(lat_count, lon_count):
    lat_steps = [lat_step for lat_step in (-1, 0, 1) if abs(lat_step) < lat_count]
    lon_steps = sorted(set((lon_step % lon_count for lon_step in (-1, 0, 1))))
    return [
        (lat_step, lon_step)
        for lat_step in lat_steps
        for lon_step in lon_steps
        if (lat_step, lon_step) != (0, 0)
    ]


def border_sides(lat_step, lon_step, lon_count):
    if lon_step == 0:
        return [(0, "last" if lat_step > 0 else "first")]
    if lat_step != 0:
        return []
    sides = []
    if lon_step == 1:
        sides.append((1, "last"))
    if lon_step == lon_count - 1:
        sides.append((1, "first"))
    return sides


def border_of(field, side):
    dim, end = side
    at = 0 if end == "first" else field.shape[dim] - 1
    return lax.index_in_dim(field, at, dim, keepdims=False)


def neighbour_mix(field, halos):
    field = field.astype(jnp.float32)
    halos = {side: halo.astype(jnp.float32) for side, halo in halos.items()}
    up = jnp.concatenate([field[1:], halos[(0, "first")][None]], axis=0)
    down = jnp.concatenate([halos[(0, "last")][None], field[:-1]], axis=0)
    right = jnp.concatenate([field[:, 1:], halos[(1, "first")][:, None]], axis=1)
    left = jnp.concatenate([halos[(1, "last")][:, None], field[:, :-1]], axis=1)
    return 0.25 * (up + down + right + left)


def one_hot(indices, count):
    return (indices[:, None] == jnp.arange(count, dtype=jnp.int32)[None, :]).astype(jnp.bfloat16)


def shared_over(blocks, axis):
    count, index = lax.axis_size(axis), lax.axis_index(axis)
    total = lax.dynamic_index_in_dim(blocks, index, 0, keepdims=False).astype(jnp.float32)
    for step in range(1, count):
        block = lax.dynamic_index_in_dim(blocks, (index + step) % count, 0, keepdims=False)
        route = [(i, (i + step) % count) for i in range(count)]
        total += lax.ppermute(block.astype(jnp.bfloat16), axis, route).astype(jnp.float32)
    return total


def column_shares(grad):
    lat_count, lon_count = lax.axis_size("lat"), lax.axis_size("lon")
    blocks = grad.reshape(lat_count, lon_count, -1, grad.shape[1])
    return shared_over(blocks.swapaxes(0, 1), "lon")


def on_device(
    grid_feat,
    mesh_in,
    w_grid,
    w_src,
    w_dst,
    b_edge,
    w_node,
    node_gain,
    mix_gain,
    send_rows,
    send_target,
    send_counts,
    local_rows,
    local_target,
    local_counts,
    cotangent,
):
    lat_count = lax.axis_size("lat")
    lon_count = lax.axis_size("lon")
    lat_index = lax.axis_index("lat")
    lon_index = lax.axis_index("lon")
    tile_a, tile_b, channels = grid_feat.shape
    mesh_a, mesh_b, latent = mesh_in.shape
    tile_rows = tile_a * tile_b
    tile_nodes = mesh_a * mesh_b
    capacity = send_rows.shape[2]
    local_slots = local_rows.shape[1]
    features = grid_feat.reshape(tile_rows, channels)
    mesh_flat = mesh_in.reshape(tile_nodes, latent)
    offsets = neighbour_offsets(lat_count, lon_count)
    slot_ids = jnp.arange(capacity, dtype=jnp.int32)
    target_codes = jnp.where(slot_ids[None, :] < send_counts[0][:, None], send_target[0] + 1, 0)
    chosen_rows, code_rows = [], []
    code_height = -(-2 * capacity // latent)
    for lat_step, lon_step in offsets:
        target_tile = (
            jnp.clip(lat_index + lat_step, 0, lat_count - 1) * lon_count
            + (lon_index + lon_step) % lon_count
        )
        chosen_rows.append(lax.dynamic_index_in_dim(send_rows[0], target_tile, 0, keepdims=False))
        codes = lax.dynamic_index_in_dim(target_codes, target_tile, 0, keepdims=False)
        halves = jnp.concatenate([codes // 256, codes % 256]).astype(jnp.bfloat16)
        halves = jnp.pad(halves, (0, code_height * latent - 2 * capacity))
        code_rows.append(halves.reshape(code_height, latent))
    sent_rows = jnp.concatenate(chosen_rows)
    mixed_cot = (mix_gain * cotangent.astype(jnp.float32)).astype(jnp.bfloat16)

    grid_pre = product(features, w_grid)
    grid_latent = jax.nn.silu(grid_pre).astype(jnp.bfloat16)
    sent_latent = product(one_hot(sent_rows, tile_rows), grid_latent).astype(jnp.bfloat16)

    arrived_blocks, arrived_codes, cot_halos = [], [], {}
    for p, (lat_step, lon_step) in enumerate(offsets):
        sides = border_sides(lat_step, lon_step, lon_count)
        pieces = [sent_latent[p * capacity : (p + 1) * capacity], code_rows[p]]
        pieces += [border_of(mixed_cot, side) for side in sides]
        came = moved(jnp.concatenate(pieces, axis=0), lat_step, lon_step)
        arrived_blocks.append(came[:capacity])
        halves = came[capacity : capacity + code_height].reshape(-1)[: 2 * capacity]
        halves = halves.astype(jnp.int32)
        arrived_codes.append(halves[:capacity] * 256 + halves[capacity:])
        at = capacity + code_height
        for side in sides:
            height = mixed_cot.shape[1 - side[0]]
            cot_halos[side] = came[at : at + height]
            at += height

    queries = (product(mesh_flat, w_dst) + b_edge).astype(jnp.bfloat16)
    here_valid = jnp.arange(local_slots, dtype=jnp.int32) < local_counts[0]
    here_targets = jnp.where(here_valid, local_target[0], -1)
    here_rows = local_rows[0]
    here_latent = product(one_hot(here_rows, tile_rows), grid_latent).astype(jnp.bfloat16)

    def edge_inputs(edge_latent, targets):
        return product(edge_latent, w_src) + product(one_hot(targets, tile_nodes), queries)

    def edge_sums(pre_edge, targets):
        return inner_rows(one_hot(targets, tile_nodes), jax.nn.silu(pre_edge).astype(jnp.bfloat16))

    here_pre = edge_inputs(here_latent, here_targets)
    here_sums = edge_sums(here_pre, here_targets)
    far_latent = jnp.concatenate(arrived_blocks, axis=0)
    far_targets = jnp.concatenate(arrived_codes) - 1
    far_pre = edge_inputs(far_latent, far_targets)
    aggregate = here_sums + edge_sums(far_pre, far_targets)

    aggregate_b = aggregate.astype(jnp.bfloat16)
    hidden = product(aggregate_b, w_node)
    active = jax.nn.silu(hidden)
    row_mean = jnp.mean(active, axis=-1, keepdims=True)
    centred = active - row_mean
    inverse_scale = lax.rsqrt(jnp.mean(centred * centred, axis=-1, keepdims=True) + LAYER_EPSILON)
    normed = centred * inverse_scale
    updated = (
        (mesh_flat.astype(jnp.float32) + normed * node_gain)
        .astype(jnp.bfloat16)
        .reshape(mesh_a, mesh_b, latent)
    )
    d_updated = cotangent.astype(jnp.float32) + neighbour_mix(mixed_cot, cot_halos)
    scaled_grad = d_updated.reshape(tile_nodes, latent) * node_gain
    d_active = inverse_scale * (
        scaled_grad
        - jnp.mean(scaled_grad, axis=-1, keepdims=True)
        - normed * jnp.mean(scaled_grad * normed, axis=-1, keepdims=True)
    )
    d_hidden = (d_active * silu_slope(hidden)).astype(jnp.bfloat16)
    d_aggregate = against_rows(d_hidden, w_node).astype(jnp.bfloat16)

    def edge_grads(pre_edge, targets):
        d_message = product(one_hot(targets, tile_nodes), d_aggregate)
        return (d_message.astype(jnp.bfloat16) * silu_slope(pre_edge)).astype(jnp.bfloat16)

    far_d_pre = edge_grads(far_pre, far_targets)
    far_d_latent = against_rows(far_d_pre, w_src).astype(jnp.bfloat16)
    d_aggregate, far_d_latent = lax.optimization_barrier((d_aggregate, far_d_latent))
    returned, halos = [], {}
    for p, (lat_step, lon_step) in enumerate(offsets):
        back = (-lat_step, (-lon_step) % lon_count)
        sides = border_sides(back[0], back[1], lon_count)
        pieces = [far_d_latent[p * capacity : (p + 1) * capacity]]
        pieces += [border_of(updated, side) for side in sides]
        came = moved(jnp.concatenate(pieces, axis=0), back[0], back[1])
        returned.append(came[:capacity])
        at = capacity
        for side in sides:
            height = updated.shape[1 - side[0]]
            halos[side] = came[at : at + height]
            at += height

    grad_node = inner_rows(d_hidden, aggregate_b)
    here_d_pre = edge_grads(here_pre, here_targets)
    grad_src = inner_rows(here_d_pre, here_latent) + inner_rows(far_d_pre, far_latent)
    d_query = inner_rows(one_hot(here_targets, tile_nodes), here_d_pre) + inner_rows(
        one_hot(far_targets, tile_nodes), far_d_pre
    )
    grad_dst = inner_rows(d_query.astype(jnp.bfloat16), mesh_flat)
    early = jnp.concatenate([grad_node, grad_src, grad_dst], axis=1).astype(jnp.bfloat16)
    early, returned, here_d_pre = lax.optimization_barrier((early, returned, here_d_pre))
    early, returned = lax.optimization_barrier((column_shares(early), returned))
    early = shared_over(early, "lat")
    here_d_latent = against_rows(here_d_pre, w_src).astype(jnp.bfloat16)
    d_grid = inner_rows(one_hot(here_rows, tile_rows), here_d_latent) + inner_rows(
        one_hot(sent_rows, tile_rows), jnp.concatenate(returned, axis=0)
    )
    d_grid_pre = (d_grid * silu_slope(grid_pre)).astype(jnp.bfloat16)
    grad_grid = inner_rows(d_grid_pre, features)
    early, grad_grid = lax.optimization_barrier((early, grad_grid))
    grad_grid = shared_over(column_shares(grad_grid), "lat").T
    grad_node = early[:, :latent].T
    grad_src = early[:, latent : 2 * latent].T
    grad_dst = early[:, 2 * latent :].T
    mesh_out = updated.astype(jnp.float32) + mix_gain * neighbour_mix(updated, halos)
    return (mesh_out, grad_grid, grad_src, grad_dst, grad_node)


def solution(mesh):
    return jax.shard_map(
        on_device,
        mesh=mesh,
        in_specs=(
            P(("dp", "lat"), "lon", None),
            P(("dp", "lat"), "lon", None),
            P(),
            P(),
            P(),
            P(),
            P(),
            P(),
            P(),
            P(("dp", "lat", "lon"), None, None),
            P(("dp", "lat", "lon"), None, None),
            P(("dp", "lat", "lon"), None),
            P(("dp", "lat", "lon"), None),
            P(("dp", "lat", "lon"), None),
            P(("dp", "lat", "lon")),
            P(("dp", "lat"), "lon", None),
        ),
        out_specs=(
            P(("dp", "lat"), "lon", None),
            P("dp", ("lat", "lon")),
            P("dp", ("lat", "lon")),
            P("dp", ("lat", "lon")),
            P("dp", ("lat", "lon")),
        ),
        check_vma=False,
    )
```
